32 devices in a mesh: row: 8 (over z, y), col: 4 (over x, core).
Axes of the slice: x: 2, y: 2, z: 4, core: 2. Of those that a mesh axis runs over, the one named last changes fastest.
Arguments:
- tokens: bfloat16 [1024, 8192], P('row', 'col'), may hold values from -6 to 6
- w_gate: bfloat16 [8192, 14336], P('col', 'row'), may hold values from -0.0625 to 0.0625
- w_up: bfloat16 [8192, 14336], P('col', 'row'), may hold values from -0.0625 to 0.0625
- w_down: bfloat16 [14336, 8192], P('row', 'col'), may hold values from -0.046875 to 0.046875
- cotangent: bfloat16 [1024, 8192], P('row', 'col'), may hold values from -0.5 to 0.5
Outputs:
- mixed: bfloat16 [1024, 8192], P('row', 'col')
- grad_gate: bfloat16 [8192, 14336], P('col', 'row')
- grad_up: bfloat16 [8192, 14336], P('col', 'row')
- grad_down: bfloat16 [14336, 8192], P('row', 'col')
The draws below stay inside these ranges and needn't reach their ends.
All inputs are finite; a program needn't handle non-finite values.
Results may differ from the reference program's by a relative error of at most 0.04.
Values may be sent and summed in bfloat16 or wider, within the bound.
A program may use at most 128 MiB of HBM per device.

```python
import jax
import jax.numpy as jnp
from jax import lax

D = 8192
FF = 14336
TOKENS = 1024
N_COL = 4


def level_of(own_key, shape, shards, low, high):
    loudness = 1.0
    for position, shards_of in shards:
        draws = jax.random.uniform(jax.random.fold_in(jax.random.fold_in(own_key, 6), position), (shards_of,), jnp.float32, low / len(shards), high / len(shards))
        loudness = loudness * jnp.repeat(jnp.exp(draws), shape[position] // shards_of).reshape((-1,) + (1,) * (len(shape) - 1 - position))
    return loudness


def noise(key, shape, deviation, limit, pieces=(), dtype=jnp.bfloat16):
    level = level_of(key, shape, pieces, -0.22, 0.18) if pieces else 1.0
    values = jax.random.normal(key, shape, jnp.float32) * deviation * level
    return jnp.minimum(jnp.maximum(values, -limit), limit).astype(dtype)


def setup_inputs(seed: int = 0) -> dict:
    splits = jax.random.split(jax.random.key(seed), 6)
    return {
        "tokens": noise(splits[0], (TOKENS, D), 1.0, 6.0, ((0, 8), (1, 4))),
        "w_gate": noise(splits[1], (D, FF), D ** -0.5, 0.0625, ((0, 4), (1, 8))),
        "w_up": noise(splits[2], (D, FF), D ** -0.5, 0.0625, ((0, 4), (1, 8))),
        "w_down": noise(splits[3], (FF, D), FF ** -0.5, 0.046875, ((0, 8), (1, 4))),
        "cotangent": noise(splits[4], (TOKENS, D), (TOKENS ** -0.5), 0.5, ((0, 8), (1, 4))),
    }


def blocked_sum(left, right_t):
    block = left.shape[1] // N_COL
    total = jnp.zeros((left.shape[0], right_t.shape[0]), jnp.float32)
    for index in range(N_COL):
        piece_left = left[:, index * block:(index + 1) * block]
        piece_right = right_t[:, index * block:(index + 1) * block]
        term = jnp.dot(piece_left, piece_right.T, preferred_element_type=jnp.float32)
        rounded = lax.optimization_barrier(term.astype(jnp.bfloat16))
        total = total + rounded.astype(jnp.float32)
    return total


def reference(tokens, w_gate, w_up, w_down, cotangent):
    gate_sum = blocked_sum(tokens, w_gate.T)
    up_sum = blocked_sum(tokens, w_up.T)
    sigmoid_gate = jax.nn.sigmoid(gate_sum)
    silu_gate = gate_sum * sigmoid_gate
    hidden = (silu_gate * up_sum).astype(jnp.bfloat16)
    mixed = jnp.dot(hidden, w_down, preferred_element_type=jnp.float32).astype(jnp.bfloat16)
    grad_down = jnp.dot(hidden.T, cotangent, preferred_element_type=jnp.float32).astype(jnp.bfloat16)
    hidden_grad = blocked_sum(cotangent, w_down)
    pre_gate = (hidden_grad * up_sum * sigmoid_gate * (1.0 + gate_sum * (1.0 - sigmoid_gate))).astype(jnp.bfloat16)
    pre_up = (hidden_grad * silu_gate).astype(jnp.bfloat16)
    grad_gate = jnp.dot(tokens.T, pre_gate, preferred_element_type=jnp.float32).astype(jnp.bfloat16)
    grad_up = jnp.dot(tokens.T, pre_up, preferred_element_type=jnp.float32).astype(jnp.bfloat16)
    return mixed, grad_gate, grad_up, grad_down
```

```python
import functools

import jax
import jax.numpy as jnp
from jax import lax
from jax.experimental import pallas as pl
from jax.experimental.pallas import tpu as pltpu
from jax.sharding import PartitionSpec as P

MESH = pl.DeviceIdType.MESH
F32 = jnp.float32
BF16 = jnp.bfloat16
Z = 4
LAG = 3


def over_tokens(left, right):
    return lax.dot_general(
        left, right, (((0,), (0,)), ((), ())), preferred_element_type=F32
    )


def nearest(at, k, n):
    other = n - 1 - at
    low = jnp.where(at <= other, at, other)
    half = (k + 1) // 2
    near = jnp.where(k % 2 == 1, at + half, at - half)
    far = jnp.where(at <= other, k, n - 1 - k)
    return jnp.where(k <= 2 * low, near, far)


def gather_kernel(
    n_row, n_col, tile,
    tok_ref, wg_ref, wu_ref, wd_ref, cot_ref,
    tok_out, cot_out, act_out,
    tok_all, cot_all, wg, wu, wd, part, pair_in, pair_sum, x_in,
    load_sem, tok_recv, cot_recv, tok_send, cot_send, keep_sem,
    pair_send, pair_recv, x_send, x_recv, act_keep, act_send, act_recv,
):
    n_y = n_row // Z
    n_x = n_col // 2
    row = lax.axis_index("row")
    col = lax.axis_index("col")
    z, y = row // n_y, row % n_y
    x, core = col // 2, col % 2
    twin = x * 2 + 1 - core
    rows = tok_ref.shape[0]
    half = rows // 2
    width = wg_ref.shape[1]
    own = pl.multiple_of(core * half, half)
    away = pl.multiple_of((1 - core) * half, half)

    loads = [
        pltpu.make_async_copy(tok_ref, tok_all.at[row], load_sem.at[0]),
        pltpu.make_async_copy(cot_ref, cot_all.at[row], load_sem.at[1]),
        pltpu.make_async_copy(wg_ref, wg, load_sem.at[2]),
        pltpu.make_async_copy(wu_ref, wu, load_sem.at[3]),
        pltpu.make_async_copy(wd_ref, wd, load_sem.at[4]),
    ]
    for load in loads:
        load.start()

    barrier = pltpu.get_barrier_semaphore()
    sides = (
        (z < Z - 1, row + n_y),
        (z > 0, row - n_y),
        (y < n_y - 1, row + 1),
        (y > 0, row - 1),
    )
    for there, who in sides:
        @pl.when(there)
        def _():
            pl.semaphore_signal(barrier, inc=1, device_id=(who, col), device_id_type=MESH)
    pl.semaphore_signal(barrier, inc=1, device_id=(row, twin), device_id_type=MESH)
    for k in range(1, n_x):
        peer = ((x + k) % n_x) * 2 + core
        pl.semaphore_signal(barrier, inc=1, device_id=(row, peer), device_id_type=MESH)
    peers = jnp.int32(n_x)
    for there, _ in sides:
        peers = peers + there.astype(jnp.int32)
    pl.semaphore_wait(barrier, peers)

    def shard(i):
        return nearest(z, i // n_y, Z) * n_y + nearest(y, i % n_y, n_y)

    def forwards(o, buf, send, recv):
        zo, yo = o // n_y, o % n_y
        whens = (
            (yo == y) & (z >= zo) & (z < Z - 1),
            (yo == y) & (z <= zo) & (z > 0),
            (y >= yo) & (y < n_y - 1),
            (y <= yo) & (y > 0),
        )
        out = []
        for d, (when, (_, who)) in enumerate(zip(whens, sides)):
            out.append((when, pltpu.make_async_remote_copy(
                src_ref=buf.at[o], dst_ref=buf.at[o],
                send_sem=send.at[o, d], recv_sem=recv.at[o],
                device_id=(who, col), device_id_type=MESH,
            )))
        return out

    def arrived(o, buf, send, recv):
        pltpu.make_async_remote_copy(
            src_ref=buf.at[o], dst_ref=buf.at[o],
            send_sem=send.at[o, 0], recv_sem=recv.at[o],
            device_id=(row, twin), device_id_type=MESH,
        ).wait_recv()

    def pair_copy(o, slot):
        return pltpu.make_async_remote_copy(
            src_ref=part.at[slot, :, pl.ds(away, half)], dst_ref=pair_in.at[o],
            send_sem=pair_send.at[o], recv_sem=pair_recv.at[o],
            device_id=(row, twin), device_id_type=MESH,
        )

    def x_copy(o, k):
        peer = ((x + k) % n_x) * 2 + core
        return pltpu.make_async_remote_copy(
            src_ref=pair_sum.at[o], dst_ref=x_in.at[o, k - 1],
            send_sem=x_send.at[o, k - 1], recv_sem=x_recv.at[o, k - 1],
            device_id=(row, peer), device_id_type=MESH,
        )

    def act_rows(o):
        return act_out.at[:, pl.ds(pl.multiple_of(o * rows + core * half, half), half)]

    def act_rows_in(o):
        return act_out.at[:, pl.ds(pl.multiple_of(o * rows + (1 - core) * half, half), half)]

    def act_local(o):
        return pltpu.make_async_copy(x_in.at[o, 0], act_rows(o), act_keep.at[o])

    def act_copy(o):
        return pltpu.make_async_remote_copy(
            src_ref=x_in.at[o, 0], dst_ref=act_rows(o),
            send_sem=act_send.at[o], recv_sem=act_recv.at[o],
            device_id=(row, twin), device_id_type=MESH,
        )

    def act_arrival(o):
        return pltpu.make_async_remote_copy(
            src_ref=x_in.at[o, 0], dst_ref=act_rows_in(o),
            send_sem=act_send.at[o], recv_sem=act_recv.at[o],
            device_id=(row, twin), device_id_type=MESH,
        )

    def keeps(o):
        to = pl.ds(pl.multiple_of(o * rows, rows), rows)
        return (
            pltpu.make_async_copy(tok_all.at[o], tok_out.at[to], keep_sem.at[o, 0]),
            pltpu.make_async_copy(cot_all.at[o], cot_out.at[to], keep_sem.at[o, 1]),
        )

    def start_forwards(o, buf, send, recv):
        for when, copy in forwards(o, buf, send, recv):
            @pl.when(when)
            def _():
                copy.start()

    def sum_pair(i):
        o, slot = shard(i), i % 2
        copy = pair_copy(o, slot)
        copy.wait()

        @pl.loop(0, width // tile)
        def _(t):
            cols = pl.ds(pl.multiple_of(t * tile, tile), tile)
            for a in range(3):
                pair_sum[o, a, :, cols] = (
                    part[slot, a, pl.ds(own, half), cols].astype(F32)
                    + pair_in[o, a, :, cols].astype(F32)
                ).astype(BF16)

        for k in range(1, n_x):
            x_copy(o, k).start()

    def finish(i):
        o = shard(i)
        for k in range(1, n_x):
            x_copy(o, k).wait_recv()

        @pl.loop(0, width // tile)
        def _(t):
            cols = pl.ds(pl.multiple_of(t * tile, tile), tile)

            def total(a):
                v = pair_sum[o, a, :, cols].astype(F32)
                for k in range(n_x - 1):
                    v = v + x_in[o, k, a, :, cols].astype(F32)
                return v

            gate, up, grad = total(0), total(1), total(2)
            s = jax.nn.sigmoid(gate)
            silu = gate * s
            x_in[o, 0, 0, :, cols] = (silu * up).astype(BF16)
            x_in[o, 0, 1, :, cols] = (grad * up * s * (1.0 + gate * (1.0 - s))).astype(BF16)
            x_in[o, 0, 2, :, cols] = (grad * silu).astype(BF16)

        act_local(o).start()
        act_copy(o).start()

    def step(i, carry):
        o = shard(i)

        @pl.when(i == 0)
        def _():
            loads[0].wait()

        @pl.when(i > 0)
        def _():
            arrived(o, tok_all, tok_send, tok_recv)

        start_forwards(o, tok_all, tok_send, tok_recv)

        @pl.when(i == 0)
        def _():
            loads[1].wait()

        @pl.when(i > 0)
        def _():
            arrived(o, cot_all, cot_send, cot_recv)

        start_forwards(o, cot_all, cot_send, cot_recv)
        for keep in keeps(o):
            keep.start()

        @pl.when(i == 0)
        def _():
            for load in loads[2:]:
                load.wait()

        slot = i % 2

        @pl.loop(0, width // tile)
        def _(t):
            cols = pl.ds(pl.multiple_of(t * tile, tile), tile)
            part[slot, 0, :, cols] = jnp.dot(
                tok_all[o], wg[:, cols], preferred_element_type=F32).astype(BF16)
            part[slot, 1, :, cols] = jnp.dot(
                tok_all[o], wu[:, cols], preferred_element_type=F32).astype(BF16)
            part[slot, 2, :, cols] = lax.dot_general(
                cot_all[o], wd[cols, :], (((1,), (1,)), ((), ())),
                preferred_element_type=F32).astype(BF16)

        pair_copy(o, slot).start()

        @pl.when(i > 0)
        def _():
            sum_pair(i - 1)

        @pl.when(i >= LAG)
        def _():
            finish(i - LAG)

        return carry

    lax.fori_loop(0, n_row, step, 0)
    sum_pair(n_row - 1)

    def rest(i, carry):
        finish(i)
        return carry

    lax.fori_loop(n_row - LAG, n_row, rest, 0)

    def drain(o, carry):
        for buf, send, recv in ((tok_all, tok_send, tok_recv), (cot_all, cot_send, cot_recv)):
            for when, copy in forwards(o, buf, send, recv):
                @pl.when(when)
                def _():
                    copy.wait_send()
        for keep in keeps(o):
            keep.wait()
        for k in range(1, n_x):
            x_copy(o, k).wait_send()
        act_local(o).wait()
        act_copy(o).wait_send()
        act_arrival(o).wait_recv()
        return carry

    lax.fori_loop(0, n_row, drain, 0)


def gather_and_act(n_row, n_col, tokens, w_gate, w_up, w_down, cotangent):
    rows, depth = tokens.shape
    width = w_gate.shape[1]
    half = rows // 2
    n_x = n_col // 2
    tile = 256 if width % 256 == 0 else 128
    dma = pltpu.SemaphoreType.DMA
    flops = 2 * n_row * rows * depth * width * 3
    return pl.pallas_call(
        functools.partial(gather_kernel, n_row, n_col, tile),
        out_shape=(
            jax.ShapeDtypeStruct((n_row * rows, depth), BF16),
            jax.ShapeDtypeStruct((n_row * rows, depth), BF16),
            jax.ShapeDtypeStruct((3, n_row * rows, width), BF16),
        ),
        in_specs=[pl.BlockSpec(memory_space=pl.ANY)] * 5,
        out_specs=[pl.BlockSpec(memory_space=pl.ANY)] * 3,
        scratch_shapes=[
            pltpu.VMEM((n_row, rows, depth), BF16),
            pltpu.VMEM((n_row, rows, depth), BF16),
            pltpu.VMEM((depth, width), BF16),
            pltpu.VMEM((depth, width), BF16),
            pltpu.VMEM((width, depth), BF16),
            pltpu.VMEM((2, 3, rows, width), BF16),
            pltpu.VMEM((n_row, 3, half, width), BF16),
            pltpu.VMEM((n_row, 3, half, width), BF16),
            pltpu.VMEM((n_row, n_x - 1, 3, half, width), BF16),
            dma((5,)),
            dma((n_row,)),
            dma((n_row,)),
            dma((n_row, 4)),
            dma((n_row, 4)),
            dma((n_row, 2)),
            dma((n_row,)),
            dma((n_row,)),
            dma((n_row, n_x - 1)),
            dma((n_row, n_x - 1)),
            dma((n_row,)),
            dma((n_row,)),
            dma((n_row,)),
        ],
        compiler_params=pltpu.CompilerParams(
            collective_id=0, has_side_effects=True, vmem_limit_bytes=60 * 1024 * 1024
        ),
        cost_estimate=pl.CostEstimate(
            flops=flops, bytes_accessed=6 * depth * width, transcendentals=0
        ),
    )(tokens, w_gate, w_up, w_down, cotangent)


def local(n_row, n_col, tokens, w_gate, w_up, w_down, cotangent):
    gathered, grad_rows, act = gather_and_act(
        n_row, n_col, tokens, w_gate, w_up, w_down, cotangent)
    hidden, pre_gate, pre_up = act[0], act[1], act[2]
    mixed_out = lax.psum_scatter(
        jnp.dot(hidden, w_down, preferred_element_type=F32).astype(BF16),
        "row",
        scatter_dimension=0,
        tiled=True,
    )
    grad_down = over_tokens(hidden, grad_rows).astype(BF16)
    grad_gate = over_tokens(gathered, pre_gate).astype(BF16)
    grad_up = over_tokens(gathered, pre_up).astype(BF16)
    return (mixed_out, grad_gate, grad_up, grad_down)


def solution(mesh):
    n_row, n_col = mesh.shape["row"], mesh.shape["col"]
    return jax.shard_map(
        functools.partial(local, n_row, n_col),
        mesh=mesh,
        in_specs=(
            P("row", "col"),
            P("col", "row"),
            P("col", "row"),
            P("row", "col"),
            P("row", "col"),
        ),
        out_specs=(P("row", "col"), P("col", "row"), P("col", "row"), P("row", "col")),
        check_vma=False,
    )
```

```python
import functools

import jax
import jax.numpy as jnp
from jax import lax
from jax.experimental import pallas as pl
from jax.experimental.pallas import tpu as pltpu
from jax.sharding import PartitionSpec as P

MESH = pl.DeviceIdType.MESH
F32 = jnp.float32
BF16 = jnp.bfloat16
Z = 4
LAG = 3
CLOSE = 3


def over_tokens(left, right):
    return lax.dot_general(
        left, right, (((0,), (0,)), ((), ())), preferred_element_type=F32
    )


def nearest(at, k, n):
    other = n - 1 - at
    low = jnp.where(at <= other, at, other)
    half = (k + 1) // 2
    near = jnp.where(k % 2 == 1, at + half, at - half)
    far = jnp.where(at <= other, k, n - 1 - k)
    return jnp.where(k <= 2 * low, near, far)


class Place:
    def __init__(self, n_row, n_col):
        self.n_y = n_row // Z
        self.n_x = n_col // 2
        self.row = lax.axis_index("row")
        self.col = lax.axis_index("col")
        self.z, self.y = self.row // self.n_y, self.row % self.n_y
        self.x, self.core = self.col // 2, self.col % 2
        self.twin = self.x * 2 + 1 - self.core
        self.sides = (
            (self.z < Z - 1, self.row + self.n_y),
            (self.z > 0, self.row - self.n_y),
            (self.y < self.n_y - 1, self.row + 1),
            (self.y > 0, self.row - 1),
        )

    def peer(self, k):
        return ((self.x + k) % self.n_x) * 2 + self.core

    def greet(self, with_rows):
        barrier = pltpu.get_barrier_semaphore()
        peers = jnp.int32(self.n_x)
        if with_rows:
            for there, who in self.sides:
                peers = peers + there.astype(jnp.int32)

                @pl.when(there)
                def _():
                    pl.semaphore_signal(
                        barrier, inc=1, device_id=(who, self.col), device_id_type=MESH)
        pl.semaphore_signal(
            barrier, inc=1, device_id=(self.row, self.twin), device_id_type=MESH)
        for k in range(1, self.n_x):
            pl.semaphore_signal(
                barrier, inc=1, device_id=(self.row, self.peer(k)), device_id_type=MESH)
        pl.semaphore_wait(barrier, peers)

    def forwards(self, o, buf, send, recv):
        zo, yo = o // self.n_y, o % self.n_y
        whens = (
            (yo == self.y) & (self.z >= zo) & (self.z < Z - 1),
            (yo == self.y) & (self.z <= zo) & (self.z > 0),
            (self.y >= yo) & (self.y < self.n_y - 1),
            (self.y <= yo) & (self.y > 0),
        )
        out = []
        for d, (when, (_, who)) in enumerate(zip(whens, self.sides)):
            out.append((when, pltpu.make_async_remote_copy(
                src_ref=buf.at[o], dst_ref=buf.at[o],
                send_sem=send.at[o, d], recv_sem=recv.at[o],
                device_id=(who, self.col), device_id_type=MESH,
            )))
        return out

    def start_forwards(self, *args):
        for when, copy in self.forwards(*args):
            @pl.when(when)
            def _():
                copy.start()

    def end_forwards(self, *args):
        for when, copy in self.forwards(*args):
            @pl.when(when)
            def _():
                copy.wait_send()

    def arrived(self, o, buf, send, recv):
        pltpu.make_async_remote_copy(
            src_ref=buf.at[o], dst_ref=buf.at[o],
            send_sem=send.at[o, 0], recv_sem=recv.at[o],
            device_id=(self.row, self.twin), device_id_type=MESH,
        ).wait_recv()


class Sums:
    def __init__(self, at, tile, n_parts, part, pair_in, pair_sum, x_in,
                 pair_send, pair_recv, x_send, x_recv):
        self.at, self.tile, self.n_parts = at, tile, n_parts
        self.part, self.pair_in, self.pair_sum, self.x_in = part, pair_in, pair_sum, x_in
        self.pair_send, self.pair_recv = pair_send, pair_recv
        self.x_send, self.x_recv = x_send, x_recv
        self.half = part.shape[2] // 2
        self.width = part.shape[3]
        self.own = pl.multiple_of(at.core * self.half, self.half)
        self.away = pl.multiple_of((1 - at.core) * self.half, self.half)

    def pair_copy(self, o, slot):
        return pltpu.make_async_remote_copy(
            src_ref=self.part.at[slot, :, pl.ds(self.away, self.half)],
            dst_ref=self.pair_in.at[o],
            send_sem=self.pair_send.at[o], recv_sem=self.pair_recv.at[o],
            device_id=(self.at.row, self.at.twin), device_id_type=MESH,
        )

    def x_copy(self, o, k):
        return pltpu.make_async_remote_copy(
            src_ref=self.pair_sum.at[o], dst_ref=self.x_in.at[o, k - 1],
            send_sem=self.x_send.at[o, k - 1], recv_sem=self.x_recv.at[o, k - 1],
            device_id=(self.at.row, self.at.peer(k)), device_id_type=MESH,
        )

    def sum_pair(self, o, slot):
        self.pair_copy(o, slot).wait()

        @pl.loop(0, self.width // self.tile)
        def _(t):
            cols = pl.ds(pl.multiple_of(t * self.tile, self.tile), self.tile)
            for a in range(self.n_parts):
                self.pair_sum[o, a, :, cols] = (
                    self.part[slot, a, pl.ds(self.own, self.half), cols].astype(F32)
                    + self.pair_in[o, a, :, cols].astype(F32)
                ).astype(BF16)

        for k in range(1, self.at.n_x):
            self.x_copy(o, k).start()

    def arrive(self, o):
        for k in range(1, self.at.n_x):
            self.x_copy(o, k).wait_recv()

    def total(self, o, a, cols):
        v = self.pair_sum[o, a, :, cols].astype(F32)
        for k in range(self.at.n_x - 1):
            v = v + self.x_in[o, k, a, :, cols].astype(F32)
        return v

    def end(self, o):
        for k in range(1, self.at.n_x):
            self.x_copy(o, k).wait_send()


class Shares:
    def __init__(self, at, rows, source, place, keep, send, recv):
        self.at, self.rows, self.half = at, rows, rows // 2
        self.source, self.place = source, place
        self.keep, self.send, self.recv = keep, send, recv

    def spot(self, o, core):
        return self.place(
            pl.ds(pl.multiple_of(o * self.rows + core * self.half, self.half), self.half))

    def local(self, o):
        return pltpu.make_async_copy(
            self.source(o), self.spot(o, self.at.core), self.keep.at[o])

    def away(self, o, core):
        return pltpu.make_async_remote_copy(
            src_ref=self.source(o), dst_ref=self.spot(o, core),
            send_sem=self.send.at[o], recv_sem=self.recv.at[o],
            device_id=(self.at.row, self.at.twin), device_id_type=MESH,
        )

    def start(self, o):
        self.local(o).start()
        self.away(o, self.at.core).start()

    def end(self, o):
        self.local(o).wait()
        self.away(o, self.at.core).wait_send()
        self.away(o, 1 - self.at.core).wait_recv()


def forward_kernel(
    n_row, n_col, tile,
    tok_ref, wg_ref, wu_ref, cot_ref,
    tok_out, cot_out, hid_out, fac_out,
    tok_all, wg, wu, part, pair_in, pair_sum, x_in, fac,
    load_sem, tok_recv, cot_recv, tok_send, cot_send, keep_sem, fac_sem,
    pair_send, pair_recv, x_send, x_recv, act_keep, act_send, act_recv,
):
    at = Place(n_row, n_col)
    rows = tok_ref.shape[0]
    width = wg_ref.shape[1]

    loads = [
        pltpu.make_async_copy(tok_ref, tok_all.at[at.row], load_sem.at[0]),
        pltpu.make_async_copy(wg_ref, wg, load_sem.at[1]),
        pltpu.make_async_copy(wu_ref, wu, load_sem.at[2]),
        pltpu.make_async_copy(cot_ref, cot_out.at[at.row], load_sem.at[3]),
    ]
    for load in loads:
        load.start()
    at.greet(True)

    sums = Sums(at, tile, 2, part, pair_in, pair_sum, x_in,
                pair_send, pair_recv, x_send, x_recv)
    shares = Shares(at, rows, lambda o: x_in.at[o, 0, 0], lambda to: hid_out.at[to],
                    act_keep, act_send, act_recv)
    tok = (tok_all, tok_send, tok_recv)
    cot = (cot_out, cot_send, cot_recv)

    def shard(i):
        return nearest(at.z, i // at.n_y, Z) * at.n_y + nearest(at.y, i % at.n_y, at.n_y)

    def keep(o):
        to = pl.ds(pl.multiple_of(o * rows, rows), rows)
        return pltpu.make_async_copy(tok_all.at[o], tok_out.at[to], keep_sem.at[o])

    def fac_copy(o):
        return pltpu.make_async_copy(fac.at[o], fac_out.at[o], fac_sem.at[o])

    def finish(i):
        o = shard(i)
        sums.arrive(o)

        @pl.loop(0, width // tile)
        def _(t):
            cols = pl.ds(pl.multiple_of(t * tile, tile), tile)
            gate, up = sums.total(o, 0, cols), sums.total(o, 1, cols)
            s = jax.nn.sigmoid(gate)
            silu = gate * s
            x_in[o, 0, 0, :, cols] = (silu * up).astype(BF16)
            fac[o, 0, :, cols] = up * s * (1.0 + gate * (1.0 - s))
            fac[o, 1, :, cols] = silu

        shares.start(o)
        fac_copy(o).start()

    def step(i, carry):
        @pl.when(i > 0)
        def _():
            sums.sum_pair(shard(i - 1), (i - 1) % 2)

        o = shard(i)

        @pl.when(i == 0)
        def _():
            loads[0].wait()

        @pl.when(i > 0)
        def _():
            at.arrived(o, *tok)

        at.start_forwards(o, *tok)
        keep(o).start()

        @pl.when(i == n_row // 2)
        def _():
            loads[3].wait()
            at.start_forwards(at.row, *cot)

        @pl.when(i == 0)
        def _():
            loads[1].wait()
            loads[2].wait()

        slot = i % 2

        @pl.loop(0, width // tile)
        def _(t):
            cols = pl.ds(pl.multiple_of(t * tile, tile), tile)
            part[slot, 0, :, cols] = jnp.dot(
                tok_all[o], wg[:, cols], preferred_element_type=F32).astype(BF16)
            part[slot, 1, :, cols] = jnp.dot(
                tok_all[o], wu[:, cols], preferred_element_type=F32).astype(BF16)

        sums.pair_copy(o, slot).start()

        @pl.when(i >= n_row - CLOSE)
        def _():
            finish(i - (n_row - CLOSE))

        return carry

    lax.fori_loop(0, n_row, step, 0)
    sums.sum_pair(shard(n_row - 1), (n_row - 1) % 2)

    def second(i, carry):
        @pl.when(i > 0)
        def _():
            o = shard(i)
            at.arrived(o, *cot)
            at.start_forwards(o, *cot)

        @pl.when(i >= CLOSE)
        def _():
            finish(i)

        return carry

    lax.fori_loop(0, n_row, second, 0)

    def drain(o, carry):
        at.end_forwards(o, *tok)
        at.end_forwards(o, *cot)
        keep(o).wait()
        fac_copy(o).wait()
        sums.end(o)
        shares.end(o)
        return carry

    lax.fori_loop(0, n_row, drain, 0)


def backward_kernel(
    n_row, n_col, tile,
    cot_ref, wd_ref, fac_ref, pre_out,
    cot_all, wd, part, pair_in, pair_sum, x_in, fac, pre,
    load_sem, cot_sem, fac_sem,
    pair_send, pair_recv, x_send, x_recv, act_keep, act_send, act_recv,
):
    at = Place(n_row, n_col)
    rows = cot_ref.shape[1]
    width = wd_ref.shape[0]

    def cot_load(o):
        return pltpu.make_async_copy(cot_ref.at[o], cot_all.at[o], cot_sem.at[o])

    def fac_load(o):
        return pltpu.make_async_copy(fac_ref.at[o], fac.at[o], fac_sem.at[o])

    load = pltpu.make_async_copy(wd_ref, wd, load_sem)
    cot_load(0).start()
    load.start()

    def begin(o, carry):
        @pl.when(o > 0)
        def _():
            cot_load(o).start()

        fac_load(o).start()
        return carry

    lax.fori_loop(0, n_row, begin, 0)
    at.greet(False)

    sums = Sums(at, tile, 1, part, pair_in, pair_sum, x_in,
                pair_send, pair_recv, x_send, x_recv)
    shares = Shares(at, rows, lambda o: pre.at[o], lambda to: pre_out.at[:, to],
                    act_keep, act_send, act_recv)

    def finish(o):
        sums.arrive(o)
        fac_load(o).wait()

        @pl.loop(0, width // tile)
        def _(t):
            cols = pl.ds(pl.multiple_of(t * tile, tile), tile)
            grad = sums.total(o, 0, cols)
            pre[o, 0, :, cols] = (grad * fac[o, 0, :, cols]).astype(BF16)
            pre[o, 1, :, cols] = (grad * fac[o, 1, :, cols]).astype(BF16)

        shares.start(o)

    def step(o, carry):
        cot_load(o).wait()

        @pl.when(o == 0)
        def _():
            load.wait()

        slot = o % 2

        @pl.loop(0, width // tile)
        def _(t):
            cols = pl.ds(pl.multiple_of(t * tile, tile), tile)
            part[slot, 0, :, cols] = lax.dot_general(
                cot_all[o], wd[cols, :], (((1,), (1,)), ((), ())),
                preferred_element_type=F32).astype(BF16)

        sums.pair_copy(o, slot).start()

        @pl.when(o > 0)
        def _():
            sums.sum_pair(o - 1, (o - 1) % 2)

        @pl.when(o >= LAG)
        def _():
            finish(o - LAG)

        return carry

    lax.fori_loop(0, n_row, step, 0)
    sums.sum_pair(n_row - 1, (n_row - 1) % 2)

    def rest(o, carry):
        finish(o)
        return carry

    lax.fori_loop(n_row - LAG, n_row, rest, 0)

    def drain(o, carry):
        sums.end(o)
        shares.end(o)
        return carry

    lax.fori_loop(0, n_row, drain, 0)


ANY = pl.BlockSpec(memory_space=pl.ANY)
DMA = pltpu.SemaphoreType.DMA


def sum_scratch(n_row, n_x, n_parts, rows, width):
    half = rows // 2
    return [
        pltpu.VMEM((2, n_parts, rows, width), BF16),
        pltpu.VMEM((n_row, n_parts, half, width), BF16),
        pltpu.VMEM((n_row, n_parts, half, width), BF16),
        pltpu.VMEM((n_row, n_x - 1, n_parts, half, width), BF16),
    ]


def sum_sems(n_row, n_x):
    return [
        DMA((n_row,)), DMA((n_row,)), DMA((n_row, n_x - 1)), DMA((n_row, n_x - 1)),
        DMA((n_row,)), DMA((n_row,)), DMA((n_row,)),
    ]


def params(number):
    return pltpu.CompilerParams(
        collective_id=number, has_side_effects=True, vmem_limit_bytes=56 * 1024 * 1024)


def forward_call(n_row, n_col, tile, tokens, w_gate, w_up, cotangent):
    rows, depth = tokens.shape
    width = w_gate.shape[1]
    n_x = n_col // 2
    total = n_row * rows
    return pl.pallas_call(
        functools.partial(forward_kernel, n_row, n_col, tile),
        out_shape=(
            jax.ShapeDtypeStruct((total, depth), BF16),
            jax.ShapeDtypeStruct((n_row, rows, depth), BF16),
            jax.ShapeDtypeStruct((total, width), BF16),
            jax.ShapeDtypeStruct((n_row, 2, rows // 2, width), F32),
        ),
        in_specs=[ANY] * 4,
        out_specs=[ANY] * 4,
        scratch_shapes=[
            pltpu.VMEM((n_row, rows, depth), BF16),
            pltpu.VMEM((depth, width), BF16),
            pltpu.VMEM((depth, width), BF16),
            *sum_scratch(n_row, n_x, 2, rows, width),
            pltpu.VMEM((n_row, 2, rows // 2, width), F32),
            DMA((4,)), DMA((n_row,)), DMA((n_row,)), DMA((n_row, 4)), DMA((n_row, 4)),
            DMA((n_row,)), DMA((n_row,)),
            *sum_sems(n_row, n_x),
        ],
        compiler_params=params(0),
        cost_estimate=pl.CostEstimate(
            flops=4 * total * depth * width, bytes_accessed=4 * depth * width,
            transcendentals=0),
    )(tokens, w_gate, w_up, cotangent)


def backward_call(n_row, n_col, tile, grad_rows, w_down, factors):
    _, rows, depth = grad_rows.shape
    width = w_down.shape[0]
    n_x = n_col // 2
    total = n_row * rows
    return pl.pallas_call(
        functools.partial(backward_kernel, n_row, n_col, tile),
        out_shape=jax.ShapeDtypeStruct((2, total, width), BF16),
        in_specs=[ANY] * 3,
        out_specs=ANY,
        scratch_shapes=[
            pltpu.VMEM((n_row, rows, depth), BF16),
            pltpu.VMEM((width, depth), BF16),
            *sum_scratch(n_row, n_x, 1, rows, width),
            pltpu.VMEM((n_row, 2, rows // 2, width), F32),
            pltpu.VMEM((n_row, 2, rows // 2, width), BF16),
            DMA, DMA((n_row,)), DMA((n_row,)),
            *sum_sems(n_row, n_x),
        ],
        compiler_params=params(1),
        cost_estimate=pl.CostEstimate(
            flops=2 * total * depth * width, bytes_accessed=2 * depth * width,
            transcendentals=0),
    )(grad_rows, w_down, factors)


def local(n_row, n_col, tokens, w_gate, w_up, w_down, cotangent):
    tile = 256 if w_gate.shape[1] % 256 == 0 else 128
    gathered, grad_rows, hidden, factors = forward_call(
        n_row, n_col, tile, tokens, w_gate, w_up, cotangent)
    terms = jnp.dot(hidden, w_down, preferred_element_type=F32).astype(BF16)
    terms, grad_rows = lax.optimization_barrier((terms, grad_rows))
    mixed_out = lax.psum_scatter(terms, "row", scatter_dimension=0, tiled=True)
    pre = backward_call(n_row, n_col, tile, grad_rows, w_down, factors)
    grad_rows = grad_rows.reshape(gathered.shape)
    grad_down = over_tokens(hidden, grad_rows).astype(BF16)
    grad_gate = over_tokens(gathered, pre[0]).astype(BF16)
    grad_up = over_tokens(gathered, pre[1]).astype(BF16)
    return (mixed_out, grad_gate, grad_up, grad_down)


def solution(mesh):
    n_row, n_col = mesh.shape["row"], mesh.shape["col"]
    return jax.shard_map(
        functools.partial(local, n_row, n_col),
        mesh=mesh,
        in_specs=(
            P("row", "col"),
            P("col", "row"),
            P("col", "row"),
            P("row", "col"),
            P("row", "col"),
        ),
        out_specs=(P("row", "col"), P("col", "row"), P("col", "row"), P("row", "col")),
        check_vma=False,
    )
```

```python
import functools

import jax
import jax.numpy as jnp
from jax import lax
from jax.experimental import pallas as pl
from jax.experimental.pallas import tpu as pltpu
from jax.sharding import PartitionSpec as P

MESH = pl.DeviceIdType.MESH
F32 = jnp.float32
BF16 = jnp.bfloat16
Z = 4
LAG = 3
CLOSE = 3


def over_tokens(left, right):
    return lax.dot_general(
        left, right, (((0,), (0,)), ((), ())), preferred_element_type=F32
    )


def nearest(at, k, n):
    other = n - 1 - at
    low = jnp.where(at <= other, at, other)
    half = (k + 1) // 2
    near = jnp.where(k % 2 == 1, at + half, at - half)
    far = jnp.where(at <= other, k, n - 1 - k)
    return jnp.where(k <= 2 * low, near, far)


class Place:
    def __init__(self, n_row, n_col):
        self.n_y = n_row // Z
        self.n_x = n_col // 2
        self.row = lax.axis_index("row")
        self.col = lax.axis_index("col")
        self.z, self.y = self.row // self.n_y, self.row % self.n_y
        self.x, self.core = self.col // 2, self.col % 2
        self.twin = self.x * 2 + 1 - self.core
        self.sides = (
            (self.z < Z - 1, self.row + self.n_y),
            (self.z > 0, self.row - self.n_y),
            (self.y < self.n_y - 1, self.row + 1),
            (self.y > 0, self.row - 1),
        )

    def peer(self, k):
        return ((self.x + k) % self.n_x) * 2 + self.core

    def shard(self, i):
        return (nearest(self.z, i // self.n_y, Z) * self.n_y
                + nearest(self.y, i % self.n_y, self.n_y))

    def greet(self):
        barrier = pltpu.get_barrier_semaphore()
        peers = jnp.int32(self.n_x)
        for there, who in self.sides:
            peers = peers + there.astype(jnp.int32)

            @pl.when(there)
            def _():
                pl.semaphore_signal(
                    barrier, inc=1, device_id=(who, self.col), device_id_type=MESH)
        pl.semaphore_signal(
            barrier, inc=1, device_id=(self.row, self.twin), device_id_type=MESH)
        for k in range(1, self.n_x):
            pl.semaphore_signal(
                barrier, inc=1, device_id=(self.row, self.peer(k)), device_id_type=MESH)
        pl.semaphore_wait(barrier, peers)

    def branches(self, o):
        zo, yo = o // self.n_y, o % self.n_y
        return (
            (yo == self.y) & (self.z >= zo) & (self.z < Z - 1),
            (yo == self.y) & (self.z <= zo) & (self.z > 0),
            (self.y >= yo) & (self.y < self.n_y - 1),
            (self.y <= yo) & (self.y > 0),
        )

    def stem(self, o):
        zo, yo = o // self.n_y, o % self.n_y
        along_y = jnp.where(yo < self.y, self.row - 1, self.row + 1)
        along_z = jnp.where(zo < self.z, self.row - self.n_y, self.row + self.n_y)
        side_y = jnp.where(yo < self.y, 2, 3)
        side_z = jnp.where(zo < self.z, 0, 1)
        return (jnp.where(yo == self.y, along_z, along_y),
                jnp.where(yo == self.y, side_z, side_y))

    def forwards(self, o, buf, send, recv):
        out = []
        for d, (when, (_, who)) in enumerate(zip(self.branches(o), self.sides)):
            out.append((when, pltpu.make_async_remote_copy(
                src_ref=buf.at[o], dst_ref=buf.at[o],
                send_sem=send.at[o, d], recv_sem=recv.at[o],
                device_id=(who, self.col), device_id_type=MESH,
            )))
        return out

    def start_forwards(self, *args):
        for when, copy in self.forwards(*args):
            @pl.when(when)
            def _():
                copy.start()

    def end_forwards(self, *args):
        for when, copy in self.forwards(*args):
            @pl.when(when)
            def _():
                copy.wait_send()

    def arrived(self, o, buf, send, recv):
        pltpu.make_async_remote_copy(
            src_ref=buf.at[o], dst_ref=buf.at[o],
            send_sem=send.at[o, 0], recv_sem=recv.at[o],
            device_id=(self.row, self.twin), device_id_type=MESH,
        ).wait_recv()


class Sums:
    def __init__(self, at, tile, n_parts, part, pair_in, pair_sum, x_in,
                 pair_send, pair_recv, x_send, x_recv):
        self.at, self.tile, self.n_parts = at, tile, n_parts
        self.part, self.pair_in, self.pair_sum, self.x_in = part, pair_in, pair_sum, x_in
        self.pair_send, self.pair_recv = pair_send, pair_recv
        self.x_send, self.x_recv = x_send, x_recv
        self.half = part.shape[2] // 2
        self.width = part.shape[3]
        self.own = pl.multiple_of(at.core * self.half, self.half)
        self.away = pl.multiple_of((1 - at.core) * self.half, self.half)

    def pair_copy(self, o, slot):
        return pltpu.make_async_remote_copy(
            src_ref=self.part.at[slot, :, pl.ds(self.away, self.half)],
            dst_ref=self.pair_in.at[o],
            send_sem=self.pair_send.at[o], recv_sem=self.pair_recv.at[o],
            device_id=(self.at.row, self.at.twin), device_id_type=MESH,
        )

    def x_copy(self, o, k):
        return pltpu.make_async_remote_copy(
            src_ref=self.pair_sum.at[o], dst_ref=self.x_in.at[o, k - 1],
            send_sem=self.x_send.at[o, k - 1], recv_sem=self.x_recv.at[o, k - 1],
            device_id=(self.at.row, self.at.peer(k)), device_id_type=MESH,
        )

    def sum_pair(self, o, slot):
        self.pair_copy(o, slot).wait()

        @pl.loop(0, self.width // self.tile)
        def _(t):
            cols = pl.ds(pl.multiple_of(t * self.tile, self.tile), self.tile)
            for a in range(self.n_parts):
                self.pair_sum[o, a, :, cols] = (
                    self.part[slot, a, pl.ds(self.own, self.half), cols].astype(F32)
                    + self.pair_in[o, a, :, cols].astype(F32)
                ).astype(BF16)

        for k in range(1, self.at.n_x):
            self.x_copy(o, k).start()

    def arrive(self, o):
        for k in range(1, self.at.n_x):
            self.x_copy(o, k).wait_recv()

    def total(self, o, a, cols):
        v = self.pair_sum[o, a, :, cols].astype(F32)
        for k in range(self.at.n_x - 1):
            v = v + self.x_in[o, k, a, :, cols].astype(F32)
        return v

    def end(self, o):
        for k in range(1, self.at.n_x):
            self.x_copy(o, k).wait_send()


class Shares:
    def __init__(self, at, rows, source, place, keep, send, recv):
        self.at, self.rows, self.half = at, rows, rows // 2
        self.source, self.place = source, place
        self.keep, self.send, self.recv = keep, send, recv

    def spot(self, o, core):
        return self.place(
            pl.ds(pl.multiple_of(o * self.rows + core * self.half, self.half), self.half))

    def local(self, o):
        return pltpu.make_async_copy(
            self.source(o), self.spot(o, self.at.core), self.keep.at[o])

    def away(self, o, core):
        return pltpu.make_async_remote_copy(
            src_ref=self.source(o), dst_ref=self.spot(o, core),
            send_sem=self.send.at[o], recv_sem=self.recv.at[o],
            device_id=(self.at.row, self.at.twin), device_id_type=MESH,
        )

    def start(self, o):
        self.local(o).start()
        self.away(o, self.at.core).start()

    def end(self, o):
        self.local(o).wait()
        self.away(o, self.at.core).wait_send()
        self.away(o, 1 - self.at.core).wait_recv()


def forward_kernel(
    n_row, n_col, tile,
    tok_ref, wg_ref, wu_ref, cot_ref,
    tok_out, cot_out, hid_out, fac_out,
    tok_all, wg, wu, part, pair_in, pair_sum, x_in, fac,
    load_sem, tok_recv, cot_recv, tok_send, cot_send, keep_sem, fac_sem,
    pair_send, pair_recv, x_send, x_recv, act_keep, act_send, act_recv,
):
    at = Place(n_row, n_col)
    rows = tok_ref.shape[0]
    width = wg_ref.shape[1]

    loads = [
        pltpu.make_async_copy(tok_ref, tok_all.at[at.row], load_sem.at[0]),
        pltpu.make_async_copy(wg_ref, wg, load_sem.at[1]),
        pltpu.make_async_copy(wu_ref, wu, load_sem.at[2]),
        pltpu.make_async_copy(cot_ref, cot_out.at[at.row], load_sem.at[3]),
    ]
    for load in loads:
        load.start()
    at.greet()

    sums = Sums(at, tile, 2, part, pair_in, pair_sum, x_in,
                pair_send, pair_recv, x_send, x_recv)
    shares = Shares(at, rows, lambda o: x_in.at[o, 0, 0], lambda to: hid_out.at[to],
                    act_keep, act_send, act_recv)
    tok = (tok_all, tok_send, tok_recv)
    cot = (cot_out, cot_send, cot_recv)

    shard = at.shard

    def keep(o):
        to = pl.ds(pl.multiple_of(o * rows, rows), rows)
        return pltpu.make_async_copy(tok_all.at[o], tok_out.at[to], keep_sem.at[o])

    def fac_copy(o):
        return pltpu.make_async_copy(fac.at[o], fac_out.at[o], fac_sem.at[o])

    def finish(i):
        o = shard(i)
        sums.arrive(o)

        @pl.loop(0, width // tile)
        def _(t):
            cols = pl.ds(pl.multiple_of(t * tile, tile), tile)
            gate, up = sums.total(o, 0, cols), sums.total(o, 1, cols)
            s = jax.nn.sigmoid(gate)
            silu = gate * s
            x_in[o, 0, 0, :, cols] = (silu * up).astype(BF16)
            fac[o, 0, :, cols] = up * s * (1.0 + gate * (1.0 - s))
            fac[o, 1, :, cols] = silu

        shares.start(o)
        fac_copy(o).start()

    def step(i, carry):
        @pl.when(i > 0)
        def _():
            sums.sum_pair(shard(i - 1), (i - 1) % 2)

        o = shard(i)

        @pl.when(i == 0)
        def _():
            loads[0].wait()

        @pl.when(i > 0)
        def _():
            at.arrived(o, *tok)

        at.start_forwards(o, *tok)
        keep(o).start()

        @pl.when(i == n_row // 2)
        def _():
            loads[3].wait()

        @pl.when(i > n_row // 2)
        def _():
            at.arrived(shard(i - n_row // 2), *cot)

        @pl.when(i >= n_row // 2)
        def _():
            at.start_forwards(shard(i - n_row // 2), *cot)

        @pl.when(i == 0)
        def _():
            loads[1].wait()
            loads[2].wait()

        slot = i % 2

        @pl.loop(0, width // tile)
        def _(t):
            cols = pl.ds(pl.multiple_of(t * tile, tile), tile)
            part[slot, 0, :, cols] = jnp.dot(
                tok_all[o], wg[:, cols], preferred_element_type=F32).astype(BF16)
            part[slot, 1, :, cols] = jnp.dot(
                tok_all[o], wu[:, cols], preferred_element_type=F32).astype(BF16)

        sums.pair_copy(o, slot).start()

        @pl.when(i >= n_row - CLOSE)
        def _():
            finish(i - (n_row - CLOSE))

        return carry

    lax.fori_loop(0, n_row, step, 0)
    sums.sum_pair(shard(n_row - 1), (n_row - 1) % 2)

    def second(i, carry):
        @pl.when(i >= n_row // 2)
        def _():
            o = shard(i)
            at.arrived(o, *cot)
            at.start_forwards(o, *cot)

        @pl.when(i >= CLOSE)
        def _():
            finish(i)

        return carry

    lax.fori_loop(0, n_row, second, 0)

    def drain(o, carry):
        at.end_forwards(o, *tok)
        at.end_forwards(o, *cot)
        keep(o).wait()
        fac_copy(o).wait()
        sums.end(o)
        shares.end(o)
        return carry

    lax.fori_loop(0, n_row, drain, 0)


def backward_kernel(
    n_row, n_col, tile,
    cot_ref, hid_ref, wd_ref, fac_ref, pre_out, mix_out,
    cot_all, hid, wd, part, pair_in, pair_sum, x_in, fac, pre, mix, mix_in,
    load_sem, mix_sem, cot_sem, hid_sem, fac_sem, mix_send, mix_recv,
    pair_send, pair_recv, x_send, x_recv, act_keep, act_send, act_recv,
):
    at = Place(n_row, n_col)
    rows, depth = cot_ref.shape[1:]
    width = wd_ref.shape[0]
    wide = 256 if depth % 256 == 0 else 128

    def cot_load(o):
        return pltpu.make_async_copy(cot_ref.at[o], cot_all.at[o], cot_sem.at[o])

    def hid_load(o):
        return pltpu.make_async_copy(
            hid_ref.at[pl.ds(pl.multiple_of(o * rows, rows), rows)], hid.at[o], hid_sem.at[o])

    def fac_load(o):
        return pltpu.make_async_copy(fac_ref.at[o], fac.at[o], fac_sem.at[o])

    load = pltpu.make_async_copy(wd_ref, wd, load_sem)
    cot_load(0).start()
    load.start()

    def begin(i, carry):
        @pl.when(i > 0)
        def _():
            cot_load(i).start()

        hid_load(at.shard(n_row - 1 - i)).start()
        fac_load(i).start()
        return carry

    lax.fori_loop(0, n_row, begin, 0)
    at.greet()

    sums = Sums(at, tile, 1, part, pair_in, pair_sum, x_in,
                pair_send, pair_recv, x_send, x_recv)
    shares = Shares(at, rows, lambda o: pre.at[o], lambda to: pre_out.at[:, to],
                    act_keep, act_send, act_recv)

    def mix_copy(o):
        who, side = at.stem(o)
        return pltpu.make_async_remote_copy(
            src_ref=mix.at[o], dst_ref=mix_in.at[o, side],
            send_sem=mix_send.at[o], recv_sem=mix_recv.at[o, side],
            device_id=(who, at.col), device_id_type=MESH,
        )

    def mix_arrived(o, d):
        pltpu.make_async_remote_copy(
            src_ref=mix.at[o], dst_ref=mix_in.at[o, d],
            send_sem=mix_send.at[o], recv_sem=mix_recv.at[o, d],
            device_id=(at.row, at.twin), device_id_type=MESH,
        ).wait_recv()

    def is_leaf(o):
        b = at.branches(o)
        return jnp.logical_not(b[0] | b[1] | b[2] | b[3])

    def mix_result():
        return pltpu.make_async_copy(mix.at[at.row], mix_out, mix_sem)

    def grow(o):
        hid_load(o).wait()

        @pl.loop(0, depth // wide)
        def _(t):
            cols = pl.ds(pl.multiple_of(t * wide, wide), wide)
            mix[o, :, cols] = jnp.dot(
                hid[o], wd[:, cols], preferred_element_type=F32).astype(BF16)

        @pl.when(is_leaf(o))
        def _():
            mix_copy(o).start()

    def join(o):
        for d, when in enumerate(at.branches(o)):
            @pl.when(when)
            def _():
                mix_arrived(o, d)

                @pl.loop(0, depth // wide)
                def _(t):
                    cols = pl.ds(pl.multiple_of(t * wide, wide), wide)
                    mix[o, :, cols] = (
                        mix[o, :, cols].astype(F32) + mix_in[o, d, :, cols].astype(F32)
                    ).astype(BF16)

        @pl.when(jnp.logical_not(is_leaf(o)) & (o != at.row))
        def _():
            mix_copy(o).start()

        @pl.when(o == at.row)
        def _():
            mix_result().start()

    def finish(o):
        sums.arrive(o)
        fac_load(o).wait()

        @pl.loop(0, width // tile)
        def _(t):
            cols = pl.ds(pl.multiple_of(t * tile, tile), tile)
            grad = sums.total(o, 0, cols)
            pre[o, 0, :, cols] = (grad * fac[o, 0, :, cols]).astype(BF16)
            pre[o, 1, :, cols] = (grad * fac[o, 1, :, cols]).astype(BF16)

        shares.start(o)

    def step(i, carry):
        @pl.when(i < n_row)
        def _():
            cot_load(i).wait()

            @pl.when(i == 0)
            def _():
                load.wait()

            slot = i % 2

            @pl.loop(0, width // tile)
            def _(t):
                cols = pl.ds(pl.multiple_of(t * tile, tile), tile)
                part[slot, 0, :, cols] = lax.dot_general(
                    cot_all[i], wd[cols, :], (((1,), (1,)), ((), ())),
                    preferred_element_type=F32).astype(BF16)

            sums.pair_copy(i, slot).start()
            grow(at.shard(n_row - 1 - i))
            sums.sum_pair(i, slot)

        @pl.when(i >= LAG)
        def _():
            join(at.shard(n_row - 1 - (i - LAG)))
            finish(i - LAG)

        return carry

    lax.fori_loop(0, n_row + LAG, step, 0)

    def drain(o, carry):
        sums.end(o)
        shares.end(o)

        @pl.when(o != at.row)
        def _():
            mix_copy(o).wait_send()

        return carry

    lax.fori_loop(0, n_row, drain, 0)
    mix_result().wait()


ANY = pl.BlockSpec(memory_space=pl.ANY)
DMA = pltpu.SemaphoreType.DMA


def sum_scratch(n_row, n_x, n_parts, rows, width):
    half = rows // 2
    return [
        pltpu.VMEM((2, n_parts, rows, width), BF16),
        pltpu.VMEM((n_row, n_parts, half, width), BF16),
        pltpu.VMEM((n_row, n_parts, half, width), BF16),
        pltpu.VMEM((n_row, n_x - 1, n_parts, half, width), BF16),
    ]


def sum_sems(n_row, n_x):
    return [
        DMA((n_row,)), DMA((n_row,)), DMA((n_row, n_x - 1)), DMA((n_row, n_x - 1)),
        DMA((n_row,)), DMA((n_row,)), DMA((n_row,)),
    ]


def params(number):
    return pltpu.CompilerParams(
        collective_id=number, has_side_effects=True, vmem_limit_bytes=56 * 1024 * 1024)


def forward_call(n_row, n_col, tile, tokens, w_gate, w_up, cotangent):
    rows, depth = tokens.shape
    width = w_gate.shape[1]
    n_x = n_col // 2
    total = n_row * rows
    return pl.pallas_call(
        functools.partial(forward_kernel, n_row, n_col, tile),
        out_shape=(
            jax.ShapeDtypeStruct((total, depth), BF16),
            jax.ShapeDtypeStruct((n_row, rows, depth), BF16),
            jax.ShapeDtypeStruct((total, width), BF16),
            jax.ShapeDtypeStruct((n_row, 2, rows // 2, width), F32),
        ),
        in_specs=[ANY] * 4,
        out_specs=[ANY] * 4,
        scratch_shapes=[
            pltpu.VMEM((n_row, rows, depth), BF16),
            pltpu.VMEM((depth, width), BF16),
            pltpu.VMEM((depth, width), BF16),
            *sum_scratch(n_row, n_x, 2, rows, width),
            pltpu.VMEM((n_row, 2, rows // 2, width), F32),
            DMA((4,)), DMA((n_row,)), DMA((n_row,)), DMA((n_row, 4)), DMA((n_row, 4)),
            DMA((n_row,)), DMA((n_row,)),
            *sum_sems(n_row, n_x),
        ],
        compiler_params=params(0),
        cost_estimate=pl.CostEstimate(
            flops=4 * total * depth * width, bytes_accessed=4 * depth * width,
            transcendentals=0),
    )(tokens, w_gate, w_up, cotangent)


def backward_call(n_row, n_col, tile, grad_rows, hidden, w_down, factors):
    _, rows, depth = grad_rows.shape
    width = w_down.shape[0]
    n_x = n_col // 2
    total = n_row * rows
    return pl.pallas_call(
        functools.partial(backward_kernel, n_row, n_col, tile),
        out_shape=(
            jax.ShapeDtypeStruct((2, total, width), BF16),
            jax.ShapeDtypeStruct((rows, depth), BF16),
        ),
        in_specs=[ANY] * 4,
        out_specs=[ANY] * 2,
        scratch_shapes=[
            pltpu.VMEM((n_row, rows, depth), BF16),
            pltpu.VMEM((n_row, rows, width), BF16),
            pltpu.VMEM((width, depth), BF16),
            *sum_scratch(n_row, n_x, 1, rows, width),
            pltpu.VMEM((n_row, 2, rows // 2, width), F32),
            pltpu.VMEM((n_row, 2, rows // 2, width), BF16),
            pltpu.VMEM((n_row, rows, depth), BF16),
            pltpu.VMEM((n_row, 4, rows, depth), BF16),
            DMA, DMA, DMA((n_row,)), DMA((n_row,)), DMA((n_row,)),
            DMA((n_row,)), DMA((n_row, 4)),
            *sum_sems(n_row, n_x),
        ],
        compiler_params=params(1),
        cost_estimate=pl.CostEstimate(
            flops=4 * total * depth * width, bytes_accessed=2 * depth * width,
            transcendentals=0),
    )(grad_rows, hidden, w_down, factors)


def local(n_row, n_col, tokens, w_gate, w_up, w_down, cotangent):
    tile = 256 if w_gate.shape[1] % 256 == 0 else 128
    gathered, grad_rows, hidden, factors = forward_call(
        n_row, n_col, tile, tokens, w_gate, w_up, cotangent)
    pre, mixed_out = backward_call(
        n_row, n_col, tile, grad_rows, hidden, w_down, factors)
    grad_rows = grad_rows.reshape(gathered.shape)
    grad_down = over_tokens(hidden, grad_rows).astype(BF16)
    grad_gate = over_tokens(gathered, pre[0]).astype(BF16)
    grad_up = over_tokens(gathered, pre[1]).astype(BF16)
    return (mixed_out, grad_gate, grad_up, grad_down)


def solution(mesh):
    n_row, n_col = mesh.shape["row"], mesh.shape["col"]
    return jax.shard_map(
        functools.partial(local, n_row, n_col),
        mesh=mesh,
        in_specs=(
            P("row", "col"),
            P("col", "row"),
            P("col", "row"),
            P("row", "col"),
            P("row", "col"),
        ),
        out_specs=(P("row", "col"), P("col", "row"), P("col", "row"), P("row", "col")),
        check_vma=False,
    )
```

```python
import functools

import jax
import jax.numpy as jnp
from jax import lax
from jax.experimental import pallas as pl
from jax.experimental.pallas import tpu as pltpu
from jax.sharding import PartitionSpec as P

MESH = pl.DeviceIdType.MESH
F32 = jnp.float32
BF16 = jnp.bfloat16
Z = 4
LAG = 3
CLOSE = 3


def over_tokens(left, right):
    return lax.dot_general(
        left, right, (((0,), (0,)), ((), ())), preferred_element_type=F32
    )


def nearest(at, k, n):
    other = n - 1 - at
    low = jnp.where(at <= other, at, other)
    half = (k + 1) // 2
    near = jnp.where(k % 2 == 1, at + half, at - half)
    far = jnp.where(at <= other, k, n - 1 - k)
    return jnp.where(k <= 2 * low, near, far)


class Place:
    def __init__(self, n_row, n_col):
        self.n_y = n_row // Z
        self.n_x = n_col // 2
        self.row = lax.axis_index("row")
        self.col = lax.axis_index("col")
        self.z, self.y = self.row // self.n_y, self.row % self.n_y
        self.x, self.core = self.col // 2, self.col % 2
        self.twin = self.x * 2 + 1 - self.core
        self.sides = (
            (self.z < Z - 1, self.row + self.n_y),
            (self.z > 0, self.row - self.n_y),
            (self.y < self.n_y - 1, self.row + 1),
            (self.y > 0, self.row - 1),
        )

    def peer(self, k):
        return ((self.x + k) % self.n_x) * 2 + self.core

    def greet(self, with_rows):
        barrier = pltpu.get_barrier_semaphore()
        peers = jnp.int32(self.n_x)
        if with_rows:
            for there, who in self.sides:
                peers = peers + there.astype(jnp.int32)

                @pl.when(there)
                def _():
                    pl.semaphore_signal(
                        barrier, inc=1, device_id=(who, self.col), device_id_type=MESH)
        pl.semaphore_signal(
            barrier, inc=1, device_id=(self.row, self.twin), device_id_type=MESH)
        for k in range(1, self.n_x):
            pl.semaphore_signal(
                barrier, inc=1, device_id=(self.row, self.peer(k)), device_id_type=MESH)
        pl.semaphore_wait(barrier, peers)

    def branches(self, o, along_z_first):
        zo, yo = o // self.n_y, o % self.n_y
        z_next = (
            (self.z >= zo) & (self.z < Z - 1),
            (self.z <= zo) & (self.z > 0),
        )
        y_next = (
            (self.y >= yo) & (self.y < self.n_y - 1),
            (self.y <= yo) & (self.y > 0),
        )
        if along_z_first:
            return tuple((yo == self.y) & when for when in z_next) + y_next
        return z_next + tuple((zo == self.z) & when for when in y_next)

    def forwards(self, o, buf, cut, along_z_first, send, recv):
        out = []
        for d, (when, (_, who)) in enumerate(zip(self.branches(o, along_z_first), self.sides)):
            out.append((when, pltpu.make_async_remote_copy(
                src_ref=buf.at[o, cut], dst_ref=buf.at[o, cut],
                send_sem=send.at[o, d], recv_sem=recv.at[o],
                device_id=(who, self.col), device_id_type=MESH,
            )))
        return out

    def start_forwards(self, *args):
        for when, copy in self.forwards(*args):
            @pl.when(when)
            def _():
                copy.start()

    def end_forwards(self, *args):
        for when, copy in self.forwards(*args):
            @pl.when(when)
            def _():
                copy.wait_send()

    def arrived(self, o, buf, cut, along_z_first, send, recv):
        pltpu.make_async_remote_copy(
            src_ref=buf.at[o, cut], dst_ref=buf.at[o, cut],
            send_sem=send.at[o, 0], recv_sem=recv.at[o],
            device_id=(self.row, self.twin), device_id_type=MESH,
        ).wait_recv()


class Sums:
    def __init__(self, at, tile, n_parts, part, pair_in, pair_sum, x_in,
                 pair_send, pair_recv, x_send, x_recv):
        self.at, self.tile, self.n_parts = at, tile, n_parts
        self.part, self.pair_in, self.pair_sum, self.x_in = part, pair_in, pair_sum, x_in
        self.pair_send, self.pair_recv = pair_send, pair_recv
        self.x_send, self.x_recv = x_send, x_recv
        self.half = part.shape[2] // 2
        self.width = part.shape[3]
        self.own = pl.multiple_of(at.core * self.half, self.half)
        self.away = pl.multiple_of((1 - at.core) * self.half, self.half)

    def pair_copy(self, o, slot):
        return pltpu.make_async_remote_copy(
            src_ref=self.part.at[slot, :, pl.ds(self.away, self.half)],
            dst_ref=self.pair_in.at[o],
            send_sem=self.pair_send.at[o], recv_sem=self.pair_recv.at[o],
            device_id=(self.at.row, self.at.twin), device_id_type=MESH,
        )

    def x_copy(self, o, k):
        return pltpu.make_async_remote_copy(
            src_ref=self.pair_sum.at[o], dst_ref=self.x_in.at[o, k - 1],
            send_sem=self.x_send.at[o, k - 1], recv_sem=self.x_recv.at[o, k - 1],
            device_id=(self.at.row, self.at.peer(k)), device_id_type=MESH,
        )

    def sum_pair(self, o, slot):
        self.pair_copy(o, slot).wait()

        @pl.loop(0, self.width // self.tile)
        def _(t):
            cols = pl.ds(pl.multiple_of(t * self.tile, self.tile), self.tile)
            for a in range(self.n_parts):
                self.pair_sum[o, a, :, cols] = (
                    self.part[slot, a, pl.ds(self.own, self.half), cols].astype(F32)
                    + self.pair_in[o, a, :, cols].astype(F32)
                ).astype(BF16)

        for k in range(1, self.at.n_x):
            self.x_copy(o, k).start()

    def arrive(self, o):
        for k in range(1, self.at.n_x):
            self.x_copy(o, k).wait_recv()

    def total(self, o, a, cols):
        v = self.pair_sum[o, a, :, cols].astype(F32)
        for k in range(self.at.n_x - 1):
            v = v + self.x_in[o, k, a, :, cols].astype(F32)
        return v

    def end(self, o):
        for k in range(1, self.at.n_x):
            self.x_copy(o, k).wait_send()


class Shares:
    def __init__(self, at, rows, source, place, keep, send, recv):
        self.at, self.rows, self.half = at, rows, rows // 2
        self.source, self.place = source, place
        self.keep, self.send, self.recv = keep, send, recv

    def spot(self, o, core):
        return self.place(
            pl.ds(pl.multiple_of(o * self.rows + core * self.half, self.half), self.half))

    def local(self, o):
        return pltpu.make_async_copy(
            self.source(o), self.spot(o, self.at.core), self.keep.at[o])

    def away(self, o, core):
        return pltpu.make_async_remote_copy(
            src_ref=self.source(o), dst_ref=self.spot(o, core),
            send_sem=self.send.at[o], recv_sem=self.recv.at[o],
            device_id=(self.at.row, self.at.twin), device_id_type=MESH,
        )

    def start(self, o):
        self.local(o).start()
        self.away(o, self.at.core).start()

    def end(self, o):
        self.local(o).wait()
        self.away(o, self.at.core).wait_send()
        self.away(o, 1 - self.at.core).wait_recv()


def forward_kernel(
    n_row, n_col, tile,
    tok_ref, wg_ref, wu_ref, cot_ref,
    tok_out, cot_out, hid_out, fac_out,
    tok_all, wg, wu, part, pair_in, pair_sum, x_in, fac,
    load_sem, tok_recv, cot_recv, alt_recv, tok_send, cot_send, alt_send, keep_sem, fac_sem,
    pair_send, pair_recv, x_send, x_recv, act_keep, act_send, act_recv,
):
    at = Place(n_row, n_col)
    rows = tok_ref.shape[0]
    width = wg_ref.shape[1]

    loads = [
        pltpu.make_async_copy(tok_ref, tok_all.at[at.row], load_sem.at[0]),
        pltpu.make_async_copy(wg_ref, wg, load_sem.at[1]),
        pltpu.make_async_copy(wu_ref, wu, load_sem.at[2]),
        pltpu.make_async_copy(cot_ref, cot_out.at[at.row], load_sem.at[3]),
    ]
    for load in loads:
        load.start()
    at.greet(True)

    sums = Sums(at, tile, 2, part, pair_in, pair_sum, x_in,
                pair_send, pair_recv, x_send, x_recv)
    shares = Shares(at, rows, lambda o: x_in.at[o, 0, 0], lambda to: hid_out.at[to],
                    act_keep, act_send, act_recv)
    most = rows - rows // 4
    tok = (tok_all, pl.ds(0, rows), True, tok_send, tok_recv)
    cot = (cot_out, pl.ds(0, most), True, cot_send, cot_recv)
    alt = (cot_out, pl.ds(most, rows - most), False, alt_send, alt_recv)

    def shard(i):
        return nearest(at.z, i // at.n_y, Z) * at.n_y + nearest(at.y, i % at.n_y, at.n_y)

    def keep(o):
        to = pl.ds(pl.multiple_of(o * rows, rows), rows)
        return pltpu.make_async_copy(tok_all.at[o], tok_out.at[to], keep_sem.at[o])

    def fac_copy(o):
        return pltpu.make_async_copy(fac.at[o], fac_out.at[o], fac_sem.at[o])

    def finish(i):
        o = shard(i)
        sums.arrive(o)

        @pl.loop(0, width // tile)
        def _(t):
            cols = pl.ds(pl.multiple_of(t * tile, tile), tile)
            gate, up = sums.total(o, 0, cols), sums.total(o, 1, cols)
            s = jax.nn.sigmoid(gate)
            silu = gate * s
            x_in[o, 0, 0, :, cols] = (silu * up).astype(BF16)
            fac[o, 0, :, cols] = up * s * (1.0 + gate * (1.0 - s))
            fac[o, 1, :, cols] = silu

        shares.start(o)
        fac_copy(o).start()

    def step(i, carry):
        @pl.when(i > 0)
        def _():
            sums.sum_pair(shard(i - 1), (i - 1) % 2)

        o = shard(i)

        @pl.when(i == 0)
        def _():
            loads[0].wait()

        @pl.when(i > 0)
        def _():
            at.arrived(o, *tok)

        at.start_forwards(o, *tok)
        keep(o).start()

        @pl.when(i == n_row // 2)
        def _():
            loads[3].wait()
            at.start_forwards(at.row, *cot)
            at.start_forwards(at.row, *alt)

        @pl.when(i == 0)
        def _():
            loads[1].wait()
            loads[2].wait()

        slot = i % 2

        @pl.loop(0, width // tile)
        def _(t):
            cols = pl.ds(pl.multiple_of(t * tile, tile), tile)
            part[slot, 0, :, cols] = jnp.dot(
                tok_all[o], wg[:, cols], preferred_element_type=F32).astype(BF16)
            part[slot, 1, :, cols] = jnp.dot(
                tok_all[o], wu[:, cols], preferred_element_type=F32).astype(BF16)

        sums.pair_copy(o, slot).start()

        @pl.when(i >= n_row - CLOSE)
        def _():
            finish(i - (n_row - CLOSE))

        return carry

    lax.fori_loop(0, n_row, step, 0)
    sums.sum_pair(shard(n_row - 1), (n_row - 1) % 2)

    def second(i, carry):
        @pl.when(i > 0)
        def _():
            o = shard(i)
            at.arrived(o, *alt)
            at.start_forwards(o, *alt)
            at.arrived(o, *cot)
            at.start_forwards(o, *cot)

        @pl.when(i >= CLOSE)
        def _():
            finish(i)

        return carry

    lax.fori_loop(0, n_row, second, 0)

    def drain(o, carry):
        at.end_forwards(o, *tok)
        at.end_forwards(o, *cot)
        at.end_forwards(o, *alt)
        keep(o).wait()
        fac_copy(o).wait()
        sums.end(o)
        shares.end(o)
        return carry

    lax.fori_loop(0, n_row, drain, 0)


def backward_kernel(
    n_row, n_col, tile,
    cot_ref, wd_ref, fac_ref, pre_out,
    cot_all, wd, part, pair_in, pair_sum, x_in, fac, pre,
    load_sem, cot_sem, fac_sem,
    pair_send, pair_recv, x_send, x_recv, act_keep, act_send, act_recv,
):
    at = Place(n_row, n_col)
    rows = cot_ref.shape[1]
    width = wd_ref.shape[0]

    def cot_load(o):
        return pltpu.make_async_copy(cot_ref.at[o], cot_all.at[o], cot_sem.at[o])

    def fac_load(o):
        return pltpu.make_async_copy(fac_ref.at[o], fac.at[o], fac_sem.at[o])

    load = pltpu.make_async_copy(wd_ref, wd, load_sem)
    cot_load(0).start()
    load.start()

    def begin(o, carry):
        @pl.when(o > 0)
        def _():
            cot_load(o).start()

        fac_load(o).start()
        return carry

    lax.fori_loop(0, n_row, begin, 0)
    at.greet(False)

    sums = Sums(at, tile, 1, part, pair_in, pair_sum, x_in,
                pair_send, pair_recv, x_send, x_recv)
    shares = Shares(at, rows, lambda o: pre.at[o], lambda to: pre_out.at[:, to],
                    act_keep, act_send, act_recv)

    def finish(o):
        sums.arrive(o)
        fac_load(o).wait()

        @pl.loop(0, width // tile)
        def _(t):
            cols = pl.ds(pl.multiple_of(t * tile, tile), tile)
            grad = sums.total(o, 0, cols)
            pre[o, 0, :, cols] = (grad * fac[o, 0, :, cols]).astype(BF16)
            pre[o, 1, :, cols] = (grad * fac[o, 1, :, cols]).astype(BF16)

        shares.start(o)

    def step(o, carry):
        cot_load(o).wait()

        @pl.when(o == 0)
        def _():
            load.wait()

        slot = o % 2

        @pl.loop(0, width // tile)
        def _(t):
            cols = pl.ds(pl.multiple_of(t * tile, tile), tile)
            part[slot, 0, :, cols] = lax.dot_general(
                cot_all[o], wd[cols, :], (((1,), (1,)), ((), ())),
                preferred_element_type=F32).astype(BF16)

        sums.pair_copy(o, slot).start()

        @pl.when(o > 0)
        def _():
            sums.sum_pair(o - 1, (o - 1) % 2)

        @pl.when(o >= LAG)
        def _():
            finish(o - LAG)

        return carry

    lax.fori_loop(0, n_row, step, 0)
    sums.sum_pair(n_row - 1, (n_row - 1) % 2)

    def rest(o, carry):
        finish(o)
        return carry

    lax.fori_loop(n_row - LAG, n_row, rest, 0)

    def drain(o, carry):
        sums.end(o)
        shares.end(o)
        return carry

    lax.fori_loop(0, n_row, drain, 0)


ANY = pl.BlockSpec(memory_space=pl.ANY)
DMA = pltpu.SemaphoreType.DMA


def sum_scratch(n_row, n_x, n_parts, rows, width):
    half = rows // 2
    return [
        pltpu.VMEM((2, n_parts, rows, width), BF16),
        pltpu.VMEM((n_row, n_parts, half, width), BF16),
        pltpu.VMEM((n_row, n_parts, half, width), BF16),
        pltpu.VMEM((n_row, n_x - 1, n_parts, half, width), BF16),
    ]


def sum_sems(n_row, n_x):
    return [
        DMA((n_row,)), DMA((n_row,)), DMA((n_row, n_x - 1)), DMA((n_row, n_x - 1)),
        DMA((n_row,)), DMA((n_row,)), DMA((n_row,)),
    ]


def params(number):
    return pltpu.CompilerParams(
        collective_id=number, has_side_effects=True, vmem_limit_bytes=56 * 1024 * 1024)


def forward_call(n_row, n_col, tile, tokens, w_gate, w_up, cotangent):
    rows, depth = tokens.shape
    width = w_gate.shape[1]
    n_x = n_col // 2
    total = n_row * rows
    return pl.pallas_call(
        functools.partial(forward_kernel, n_row, n_col, tile),
        out_shape=(
            jax.ShapeDtypeStruct((total, depth), BF16),
            jax.ShapeDtypeStruct((n_row, rows, depth), BF16),
            jax.ShapeDtypeStruct((total, width), BF16),
            jax.ShapeDtypeStruct((n_row, 2, rows // 2, width), F32),
        ),
        in_specs=[ANY] * 4,
        out_specs=[ANY] * 4,
        scratch_shapes=[
            pltpu.VMEM((n_row, rows, depth), BF16),
            pltpu.VMEM((depth, width), BF16),
            pltpu.VMEM((depth, width), BF16),
            *sum_scratch(n_row, n_x, 2, rows, width),
            pltpu.VMEM((n_row, 2, rows // 2, width), F32),
            DMA((4,)), DMA((n_row,)), DMA((n_row,)), DMA((n_row,)),
            DMA((n_row, 4)), DMA((n_row, 4)), DMA((n_row, 4)),
            DMA((n_row,)), DMA((n_row,)),
            *sum_sems(n_row, n_x),
        ],
        compiler_params=params(0),
        cost_estimate=pl.CostEstimate(
            flops=4 * total * depth * width, bytes_accessed=4 * depth * width,
            transcendentals=0),
    )(tokens, w_gate, w_up, cotangent)


def backward_call(n_row, n_col, tile, grad_rows, w_down, factors):
    _, rows, depth = grad_rows.shape
    width = w_down.shape[0]
    n_x = n_col // 2
    total = n_row * rows
    return pl.pallas_call(
        functools.partial(backward_kernel, n_row, n_col, tile),
        out_shape=jax.ShapeDtypeStruct((2, total, width), BF16),
        in_specs=[ANY] * 3,
        out_specs=ANY,
        scratch_shapes=[
            pltpu.VMEM((n_row, rows, depth), BF16),
            pltpu.VMEM((width, depth), BF16),
            *sum_scratch(n_row, n_x, 1, rows, width),
            pltpu.VMEM((n_row, 2, rows // 2, width), F32),
            pltpu.VMEM((n_row, 2, rows // 2, width), BF16),
            DMA, DMA((n_row,)), DMA((n_row,)),
            *sum_sems(n_row, n_x),
        ],
        compiler_params=params(1),
        cost_estimate=pl.CostEstimate(
            flops=2 * total * depth * width, bytes_accessed=2 * depth * width,
            transcendentals=0),
    )(grad_rows, w_down, factors)


def local(n_row, n_col, tokens, w_gate, w_up, w_down, cotangent):
    tile = 256 if w_gate.shape[1] % 256 == 0 else 128
    gathered, grad_rows, hidden, factors = forward_call(
        n_row, n_col, tile, tokens, w_gate, w_up, cotangent)
    terms = jnp.dot(hidden, w_down, preferred_element_type=F32).astype(BF16)
    terms, grad_rows = lax.optimization_barrier((terms, grad_rows))
    mixed_out = lax.psum_scatter(terms, "row", scatter_dimension=0, tiled=True)
    pre = backward_call(n_row, n_col, tile, grad_rows, w_down, factors)
    grad_rows = grad_rows.reshape(gathered.shape)
    grad_down = over_tokens(hidden, grad_rows).astype(BF16)
    grad_gate = over_tokens(gathered, pre[0]).astype(BF16)
    grad_up = over_tokens(gathered, pre[1]).astype(BF16)
    return (mixed_out, grad_gate, grad_up, grad_down)


def solution(mesh):
    n_row, n_col = mesh.shape["row"], mesh.shape["col"]
    return jax.shard_map(
        functools.partial(local, n_row, n_col),
        mesh=mesh,
        in_specs=(
            P("row", "col"),
            P("col", "row"),
            P("col", "row"),
            P("row", "col"),
            P("row", "col"),
        ),
        out_specs=(P("row", "col"), P("col", "row"), P("col", "row"), P("row", "col")),
        check_vma=False,
    )
```
